32 devices in a mesh: rows: 8 (over y, x, core), cols: 4 (over z).
Axes of the slice: x: 2, y: 2, z: 4, core: 2. Of those that a mesh axis runs over, the one named last changes fastest.
Arguments:
- inputs: bfloat16 [8192, 2048], P(('rows', 'cols')), may hold values from -6 to 6
- lengths: int32 [8], P('rows'), may hold values from 256 to 1024, as said below
- gain_one: float32 [2048], replicated, may hold values from 0.1 to 1.9
- shift_one: float32 [2048], replicated, may hold values from -3 to 3
- projection: bfloat16 [2048, 3, 2048], P('rows', None, 'cols'), may hold values from -0.125 to 0.125
- query_bias: float32 [2048], P('cols'), may hold values from -3 to 3
- value_bias: float32 [2048], P('cols'), may hold values from -3 to 3
- out_weight: bfloat16 [2048, 2048], P('cols', 'rows'), may hold values from -0.5 to 0.5
- out_bias: float32 [2048], replicated, may hold values from -3 to 3
- gain_two: float32 [2048], replicated, may hold values from 0.1 to 1.9
- shift_two: float32 [2048], replicated, may hold values from -3 to 3
- up_weight: bfloat16 [2048, 8192], P('rows', 'cols'), may hold values from -0.125 to 0.125
- up_bias: float32 [8192], P('cols'), may hold values from -3 to 3
- down_weight: bfloat16 [8192, 2048], P('cols', 'rows'), may hold values from -0.0625 to 0.0625
- down_bias: float32 [2048], replicated, may hold values from -3 to 3
- cotangent: bfloat16 [8192, 2048], P(('rows', 'cols')), may hold values from -6 to 6
Outputs:
- output: bfloat16 [8192, 2048], P(('rows', 'cols'))
- inputs_grad: float32 [8192, 2048], P(('rows', 'cols'))
- gain_one_grad: float32 [2048], replicated
- shift_one_grad: float32 [2048], replicated
- projection_grad: float32 [2048, 3, 2048], P('rows', None, 'cols')
- query_bias_grad: float32 [2048], P('cols')
- value_bias_grad: float32 [2048], P('cols')
- out_weight_grad: float32 [2048, 2048], P('cols', 'rows')
- out_bias_grad: float32 [2048], replicated
- gain_two_grad: float32 [2048], replicated
- shift_two_grad: float32 [2048], replicated
- up_weight_grad: float32 [2048, 8192], P('rows', 'cols')
- up_bias_grad: float32 [8192], P('cols')
- down_weight_grad: float32 [8192, 2048], P('cols', 'rows')
- down_bias_grad: float32 [2048], replicated
The draws below stay inside these ranges and needn't reach their ends.
Inputs may be any that keep to these rules, and one draw needn't show every extreme that they name: `lengths`: one sequence has all 1024 slots live and another a quarter of them.
All inputs are finite; a program needn't handle non-finite values.
Results may differ from the reference program's by a relative error of at most 0.02.
Values may be sent and summed in bfloat16 or wider, within the bound.
A program may use at most 256 MiB of HBM per device.

```python
import math
from functools import partial
import jax
import jax.numpy as jnp
from jax import lax

D = 2048
HEADS = 32
HEAD_DIM = 64
FF = 8192
SEQ_LEN = 1024
NSEQ = 8
TOKENS = 8192


def draw_lengths(key, part):
    first_key, second_key = jax.random.split(jax.random.fold_in(key, 17))
    drawn = jax.random.randint(first_key, (NSEQ,), SEQ_LEN // 4, SEQ_LEN + 1)
    chosen = jax.random.randint(second_key, (), 0, NSEQ)
    slots = jnp.arange(NSEQ)
    drawn = jnp.where(slots == chosen, SEQ_LEN, drawn)
    drawn = jnp.where(slots == (chosen + 1) % NSEQ, SEQ_LEN // 4, drawn)
    return drawn.astype(jnp.int32)


def shard_levels(own_key, shape, shards, smallest, largest):
    level = 1.0
    for axis_at, parts in shards:
        draws = jax.random.uniform(jax.random.fold_in(jax.random.fold_in(own_key, 6), axis_at), (parts,), jnp.float32, smallest / len(shards), largest / len(shards))
        level = level * jnp.repeat(jnp.exp(draws), shape[axis_at] // parts).reshape((-1,) + (1,) * (len(shape) - 1 - axis_at))
    return level


def normal_values(own_key, extent, scale, bound, cuts=(), kind=jnp.bfloat16):
    values = scale * jax.random.normal(own_key, extent, jnp.float32)
    if cuts:
        values = values * shard_levels(own_key, extent, cuts, -0.22, 0.18)
    return jnp.clip(values, -bound, bound).astype(kind)


def setup_inputs(seed: int = 0) -> dict:
    splits = jax.random.split(jax.random.key(seed), 17)
    return {
        "inputs": normal_values(splits[0], (TOKENS, D), 1.0, 6.0, ((0, 32),)),
        "lengths": draw_lengths(jax.random.fold_in(splits[16], 71), 0),
        "gain_one": jnp.clip(1.0 + 0.18 * jax.random.normal(splits[2], (D,), jnp.float32), 0.1, 1.9),
        "shift_one": normal_values(splits[3], (D,), 0.3, 3.0, (), jnp.float32),
        "projection": normal_values(splits[4], (D, 3, D), D ** -0.5, 0.125, ((0, 8), (2, 4))),
        "query_bias": normal_values(splits[5], (D,), 0.5, 3.0, ((0, 4),), jnp.float32),
        "value_bias": normal_values(splits[6], (D,), 0.5, 3.0, ((0, 4),), jnp.float32),
        "out_weight": normal_values(splits[7], (D, D), (D // 16) ** -0.5, 0.5, ((0, 4), (1, 8))),
        "out_bias": normal_values(splits[8], (D,), 0.3, 3.0, (), jnp.float32),
        "gain_two": jnp.clip(1.0 + 0.18 * jax.random.normal(splits[9], (D,), jnp.float32), 0.1, 1.9),
        "shift_two": normal_values(splits[10], (D,), 0.3, 3.0, (), jnp.float32),
        "up_weight": normal_values(splits[11], (D, FF), D ** -0.5, 0.125, ((0, 8), (1, 4))),
        "up_bias": normal_values(splits[12], (FF,), 0.5, 3.0, ((0, 4),), jnp.float32),
        "down_weight": normal_values(splits[13], (FF, D), FF ** -0.5, 0.0625, ((0, 4), (1, 8))),
        "down_bias": normal_values(splits[14], (D,), 0.3, 3.0, (), jnp.float32),
        "cotangent": normal_values(splits[15], (TOKENS, D), 1.0, 6.0, ((0, 32),)),
    }


@jax.custom_vjp
def low(v):
    return lax.optimization_barrier(v.astype(jnp.bfloat16)).astype(jnp.float32)

@jax.custom_vjp
def low_back(v):
    return v

def low_keep(v):
    return (low(v), None)

def low_pass(kept, grad):
    return (grad,)

def back_keep(v):
    return (v, None)

def back_low(kept, grad):
    return (low(grad),)
low.defvjp(low_keep, low_pass)
low_back.defvjp(back_keep, back_low)
precise = lax.Precision.HIGHEST
epsilon = 1e-05

def normalize(values, gain_row, shift_row):
    center = lax.optimization_barrier(jnp.mean(values, axis=-1, keepdims=True))
    centred = values - center
    spread = lax.optimization_barrier(jnp.mean(centred * centred, axis=-1, keepdims=True))
    return centred * lax.rsqrt(spread + epsilon) * gain_row + shift_row

def attend_block(members):
    queries, key_rows, values, seq_length, head_ids = members
    scaling = HEAD_DIM ** (-0.5)
    positions = jnp.arange(SEQ_LEN)
    offset = (positions[None, :] - positions[:, None]).astype(jnp.float32)
    slopes = jnp.exp2(-8.0 * (head_ids + 1).astype(jnp.float32) / HEADS)
    scores = jnp.einsum('qhd,khd->hqk', queries, key_rows, precision=precise) * scaling
    scores = low_back(scores + slopes[:, None, None] * offset[None, :, :])
    allowed = (positions[None, :] <= positions[:, None]) & (positions[None, :] < seq_length)
    scores = jnp.where(allowed[None], scores, -1000000000.0)
    highest = lax.optimization_barrier(jnp.max(scores, axis=-1, keepdims=True))
    raised = jnp.exp(scores - highest)
    weights = low(raised / lax.optimization_barrier(jnp.sum(raised, axis=-1, keepdims=True)))
    return jnp.einsum('hqk,khd->qhd', weights, values, precision=precise)

def attention(queries, key_rows, values, lengths):
    group_size = math.gcd(HEADS, 8)
    blocks = HEADS // group_size

    def by_group(rows):
        shaped = rows.reshape(NSEQ, SEQ_LEN, blocks, group_size, HEAD_DIM).transpose(0, 2, 1, 3, 4)
        return shaped.reshape(NSEQ * blocks, SEQ_LEN, group_size, HEAD_DIM)
    head_ids = jnp.tile(jnp.arange(HEADS, dtype=jnp.int32).reshape(blocks, group_size), (NSEQ, 1))
    seq_lengths = jnp.repeat(lengths, blocks)
    result = lax.map(jax.checkpoint(attend_block), (by_group(queries), by_group(key_rows), by_group(values), seq_lengths, head_ids))
    shaped = result.reshape(NSEQ, blocks, SEQ_LEN, group_size, HEAD_DIM).transpose(0, 2, 1, 3, 4)
    return shaped.reshape(TOKENS, D)

def forward(lengths, inputs, gain_one, shift_one, projection, query_bias, value_bias, out_weight, out_bias, gain_two, shift_two, up_weight, up_bias, down_weight, down_bias):
    positions = jnp.arange(SEQ_LEN)
    live_rows = (positions[None, :] < lengths[:, None]).astype(jnp.float32).reshape(TOKENS, 1)
    h_one = low(normalize(inputs, gain_one, shift_one))
    projected = jnp.dot(h_one, projection.reshape(D, 3 * D), precision=precise).reshape(TOKENS, 3, D)
    queries = low_back(low(projected[:, 0, :] + query_bias))
    key_rows = low_back(low(projected[:, 1, :]))
    values = low_back(low(projected[:, 2, :] + value_bias))
    attended = low_back(low(attention(queries, key_rows, values, lengths)))
    branch = low_back(jnp.dot(attended, out_weight, precision=precise) + out_bias)
    middle = inputs + live_rows * branch
    h_two = low(normalize(middle, gain_two, shift_two))
    before = low_back(jnp.dot(h_two, up_weight, precision=precise) + up_bias)
    active = low(jax.nn.gelu(before, approximate=False))
    dense_out = low_back(jnp.dot(active, down_weight, precision=precise) + down_bias)
    return middle + live_rows * dense_out

def reference(inputs, lengths, gain_one, shift_one, projection, query_bias, value_bias, out_weight, out_bias, gain_two, shift_two, up_weight, up_bias, down_weight, down_bias, cotangent):
    floats = tuple((member.astype(jnp.float32) for member in (inputs, gain_one, shift_one, projection, query_bias, value_bias, out_weight, out_bias, gain_two, shift_two, up_weight, up_bias, down_weight, down_bias)))
    result, pullback = jax.vjp(partial(forward, lengths), *floats)
    gradients = pullback(cotangent.astype(jnp.float32))
    return (result.astype(jnp.bfloat16), gradients[0], gradients[1], gradients[2], gradients[3], gradients[4], gradients[5], gradients[6], gradients[7], gradients[8], gradients[9], gradients[10], gradients[11], gradients[12], gradients[13])
```

```python
import functools
import math

import jax
import jax.numpy as jnp
from jax import lax
from jax.experimental import pallas as pl
from jax.experimental.pallas import tpu as pltpu
from jax.sharding import PartitionSpec as P

HEADS = 32
HEAD_DIM = 64
LOG2E = 1.4426950408889634
LOW = -1.0e9
epsilon = 1e-05
bf16 = jnp.bfloat16
f32 = jnp.float32
MESH = pl.DeviceIdType.MESH
VM = pl.BlockSpec(memory_space=pltpu.VMEM)
SM = pl.BlockSpec(memory_space=pltpu.SMEM)
HB = pl.BlockSpec(memory_space=pl.ANY)


def nn(a, b):
    return lax.dot_general(a, b, (((1,), (0,)), ((), ())), preferred_element_type=f32)


def nt(a, b):
    return lax.dot_general(a, b, (((1,), (1,)), ((), ())), preferred_element_type=f32)


def tn(a, b):
    return lax.dot_general(a, b, (((0,), (0,)), ((), ())), preferred_element_type=f32)


def normalize(values):
    center = jnp.mean(values, axis=-1, keepdims=True)
    centred = values - center
    spread = jnp.mean(centred * centred, axis=-1, keepdims=True)
    inverse = lax.rsqrt(spread + epsilon)
    return centred * inverse, inverse


def norm_back(grad_rows, normed, inverse, gain_row):
    scaled = grad_rows * gain_row
    first_mean = jnp.mean(scaled, axis=-1, keepdims=True)
    second = jnp.mean(scaled * normed, axis=-1, keepdims=True)
    return inverse * (scaled - first_mean - normed * second)


def live_mask(length, start, rows):
    return (start + lax.broadcasted_iota(jnp.int32, (rows, 1), 0) < length).astype(f32)


def line_barrier(r, c, n):
    barrier = pltpu.get_barrier_semaphore()

    @pl.when(c > 0)
    def _():
        pl.semaphore_signal(barrier, inc=1, device_id=(r, c - 1), device_id_type=MESH)

    @pl.when(c < n - 1)
    def _():
        pl.semaphore_signal(barrier, inc=1, device_id=(r, c + 1), device_id_type=MESH)

    pl.semaphore_wait(barrier, (c > 0).astype(jnp.int32) + (c < n - 1).astype(jnp.int32))


class LineGather:
    def __init__(self, r, c, n, own, full, sends, recvs):
        self.r, self.c, self.n, self.own, self.full = r, c, n, own, full
        self.sends, self.recvs = sends, recvs

    def copy(self, way, k, j):
        block = self.c - k if way == 0 else self.c + k
        to = self.c + 1 if way == 0 else self.c - 1
        src = self.own(j) if k == 0 else self.full(block, j)
        return pltpu.make_async_remote_copy(
            src_ref=src,
            dst_ref=self.full(block, j),
            send_sem=self.sends.at[way, k, j],
            recv_sem=self.recvs.at[way, k, j],
            device_id=(self.r, to),
            device_id_type=MESH,
        )

    def arrives(self, way, k):
        return self.c - 1 - k >= 0 if way == 0 else self.c + 1 + k <= self.n - 1

    def leaves(self, way, k):
        if way == 0:
            return (self.c - k >= 0) & (self.c < self.n - 1)
        return (self.c + k <= self.n - 1) & (self.c > 0)

    def landed(self, way, k, j):
        block = self.c - 1 - k if way == 0 else self.c + 1 + k
        to = self.c + 1 if way == 0 else self.c - 1
        return pltpu.make_async_remote_copy(
            src_ref=self.full(block, j),
            dst_ref=self.full(block, j),
            send_sem=self.sends.at[way, k, j],
            recv_sem=self.recvs.at[way, k, j],
            device_id=(self.r, to),
            device_id_type=MESH,
        )

    def step(self, k, j):
        for way in (0, 1):
            if k > 0:
                pl.when(self.arrives(way, k - 1))(
                    lambda way=way: self.landed(way, k - 1, j).wait_recv()
                )
            if k < self.n - 1:
                pl.when(self.leaves(way, k))(lambda way=way: self.copy(way, k, j).start())

    def drain(self, j):
        for way in (0, 1):
            for k in range(self.n - 1):
                pl.when(self.leaves(way, k))(
                    lambda way=way, k=k: self.copy(way, k, j).wait_send()
                )


class LineScatter:
    def __init__(self, r, c, n, part, land, sends, recvs):
        self.r, self.c, self.n, self.part, self.land = r, c, n, part, land
        self.sends, self.recvs = sends, recvs

    def copy(self, way, b, j):
        to = self.c + 1 if way == 0 else self.c - 1
        return pltpu.make_async_remote_copy(
            src_ref=self.part(b, j),
            dst_ref=self.land(way, b, j),
            send_sem=self.sends.at[way, b, j],
            recv_sem=self.recvs.at[way, b, j],
            device_id=(self.r, to),
            device_id_type=MESH,
        )

    def first(self, way, b, j):
        end = 0 if way == 0 else self.n - 1
        pl.when((self.c == end) & (self.c != b))(lambda: self.copy(way, b, j).start())

    def middle(self, way, b, j):
        here = (self.c > 0) & (self.c < b) if way == 0 else (self.c < self.n - 1) & (self.c > b)

        @pl.when(here)
        def _():
            self.copy(way, b, j).wait_recv()
            part = self.part(b, j)
            part[...] = (part[...].astype(f32) + self.land(way, b, j)[...].astype(f32)).astype(bf16)
            self.copy(way, b, j).start()

    def last(self, j, total):
        total[...] = self.part(self.c, j)[...].astype(f32)
        for way in (0, 1):

            @pl.when(self.c > 0 if way == 0 else self.c < self.n - 1)
            def _(way=way):
                self.copy(way, self.c, j).wait_recv()
                total[...] += self.land(way, self.c, j)[...].astype(f32)

    def drain(self, b, j):
        for way in (0, 1):
            if way == 0:
                sent = (self.c < b) & (self.c < self.n - 1)
            else:
                sent = (self.c > b) & (self.c > 0)
            pl.when(sent)(lambda way=way: self.copy(way, b, j).wait_send())


def scatter_order(n):
    return [(way, n - 1 - k if way == 0 else k) for k in range(n - 1) for way in (0, 1)]


def pieces_of(rows):
    return max(1, rows // 64)


def gather_kernel(n, pieces, x_ref, gain_ref, shift_ref, full_ref, own, sends, recvs, local_sem):
    r, c = lax.axis_index("rows"), lax.axis_index("cols")
    tok = x_ref.shape[0]
    sub = tok // pieces

    def full(b, j):
        return full_ref.at[pl.ds(b * tok + j * sub, sub)]

    gather = LineGather(r, c, n, lambda j: own.at[pl.ds(j * sub, sub)], full, sends, recvs)
    line_barrier(r, c, n)
    for j in range(pieces):
        rows = pl.ds(j * sub, sub)
        normed, _ = normalize(x_ref[rows].astype(f32))
        own[rows] = (normed * gain_ref[...] + shift_ref[...]).astype(bf16)
        gather.step(0, j)
    keep = pltpu.make_async_copy(own, full_ref.at[pl.ds(c * tok, tok)], local_sem)
    keep.start()
    for k in range(1, n):
        for j in range(pieces):
            gather.step(k, j)
    for j in range(pieces):
        gather.drain(j)
    keep.wait()


def gather_normed(n, x, gain, shift):
    tok, width = x.shape
    pieces = pieces_of(tok)
    return pl.pallas_call(
        functools.partial(gather_kernel, n, pieces),
        out_shape=jax.ShapeDtypeStruct((n * tok, width), bf16),
        in_specs=[VM, VM, VM],
        out_specs=HB,
        scratch_shapes=[
            pltpu.VMEM((tok, width), bf16),
            pltpu.SemaphoreType.DMA((2, n - 1, pieces)),
            pltpu.SemaphoreType.DMA((2, n - 1, pieces)),
            pltpu.SemaphoreType.DMA,
        ],
        compiler_params=pltpu.CompilerParams(
            collective_id=1, has_side_effects=True, vmem_limit_bytes=24 * 2**20
        ),
        cost_estimate=pl.CostEstimate(
            flops=10 * tok * width, bytes_accessed=60 * 2**20, transcendentals=0
        ),
        name="gather_normed",
    )(x, gain, shift)


def key_bias(slope, length, keys):
    at = lax.broadcasted_iota(jnp.int32, (1, keys), 1)
    return jnp.where(at < length, slope * LOG2E * at.astype(f32), LOW)


def masked_scores(query, keys, bias, tok, start):
    scores = nt(query, keys) * LOG2E + bias
    row = lax.broadcasted_iota(jnp.int32, (tok, tok), 0)
    col = lax.broadcasted_iota(jnp.int32, (tok, tok), 1)
    tail = jnp.where(col <= row, scores[:, start:], LOW)
    if start == 0:
        return tail
    return jnp.concatenate([scores[:, :start], tail], axis=1)


def attend_block(tok, b, q_ref, k_ref, v_ref, att_ref, lse_ref, slopes_ref, length):
    pairs = q_ref.shape[1] // 128
    extent = (b + 1) * tok
    rows = pl.ds(b * tok, tok)
    lane = lax.broadcasted_iota(jnp.int32, (tok, 128), 1)

    def pair(p, lse_all):
        lanes = pl.ds(pl.multiple_of(p * 128, 128), 128)
        query = q_ref[rows, lanes]
        keys = k_ref[pl.ds(0, extent), lanes]
        values = v_ref[pl.ds(0, extent), lanes]
        results = []
        for u in (0, 1):
            mine = (lane < 64) if u == 0 else (lane >= 64)
            bias = key_bias(slopes_ref[0, 2 * p + u], length, extent)
            scores = masked_scores(
                jnp.where(mine, query, jnp.zeros_like(query)), keys, bias, tok, b * tok
            )
            highest = jnp.max(scores, axis=1, keepdims=True)
            raised = jnp.exp2(scores - highest)
            summed = jnp.sum(raised, axis=1, keepdims=True)
            results.append(nn(raised.astype(bf16), values) * (1.0 / summed))
            total = highest + jnp.log2(summed)
            lse_all = jnp.where(lane == 2 * p + u, total, lse_all)
        att_ref[rows, lanes] = jnp.where(lane < 64, results[0], results[1]).astype(bf16)
        return lse_all

    lse_ref[rows, :] = lax.fori_loop(0, pairs, pair, jnp.zeros((tok, 128), f32))


def attention_kernel(
    n,
    pieces,
    h_ref,
    proj_ref,
    qb_ref,
    vb_ref,
    slopes_ref,
    length_ref,
    outw_ref,
    x_ref,
    outb_ref,
    gain_ref,
    shift_ref,
    cot_ref,
    q_ref,
    k_ref,
    v_ref,
    att_ref,
    lse_ref,
    mid_ref,
    h2_ref,
    dense_ref,
    own,
    part_ref,
    land_ref,
    total,
    g_sends,
    g_recvs,
    s_sends,
    s_recvs,
    local_sem,
):
    r, c = lax.axis_index("rows"), lax.axis_index("cols")
    tok = x_ref.shape[0]
    width = x_ref.shape[1]
    sub = tok // pieces
    length = length_ref[0]

    gather = LineGather(
        r,
        c,
        n,
        lambda j: own.at[pl.ds(j * sub, sub)],
        lambda b, j: dense_ref.at[pl.ds(b * tok + j * sub, sub)],
        g_sends,
        g_recvs,
    )
    scatter = LineScatter(
        r,
        c,
        n,
        lambda b, j: part_ref.at[pl.ds(b * tok + j * sub, sub)],
        lambda way, b, j: land_ref.at[way, pl.ds(b * tok + j * sub, sub)],
        s_sends,
        s_recvs,
    )
    line_barrier(r, c, n)
    for j in range(pieces):
        rows = pl.ds(j * sub, sub)
        live = live_mask(length, c * tok + j * sub, sub)
        own[rows] = (live * cot_ref[rows].astype(f32)).astype(bf16)
        gather.step(0, j)
    keep = pltpu.make_async_copy(own, dense_ref.at[pl.ds(c * tok, tok)], local_sem)
    keep.start()

    def project(b, _):
        rows = pl.ds(pl.multiple_of(b * tok, tok), tok)
        h = h_ref[rows]
        q_ref[rows] = (nn(h, proj_ref[0]) + qb_ref[...]).astype(bf16) * jnp.asarray(0.125, bf16)
        k_ref[rows] = nn(h, proj_ref[1]).astype(bf16)
        v_ref[rows] = (nn(h, proj_ref[2]) + vb_ref[...]).astype(bf16)
        return 0

    lax.fori_loop(0, n, project, 0)

    forward = [(k, j) for k in range(1, n) for j in range(pieces)]
    order = []
    low, high = 0, n - 1
    while low <= high:
        order.append(high)
        if low != high:
            order.append(low)
        low, high = low + 1, high - 1
    for at, b in enumerate(order):
        attend_block(tok, b, q_ref, k_ref, v_ref, att_ref, lse_ref, slopes_ref, length)
        att = att_ref[pl.ds(b * tok, tok)]
        for w in range(width // 512):
            lanes = pl.ds(w * 512, 512)
            part_ref[pl.ds(b * tok, tok), lanes] = nn(att, outw_ref[:, lanes]).astype(bf16)
        for j in range(pieces):
            scatter.first(0, b, j)
            scatter.first(1, b, j)
        if at < len(order) - 1:
            for _ in range(pieces // 2 if n > 2 else 0):
                k, j = forward.pop(0)
                gather.step(k, j)
    for way, b in scatter_order(n):
        for j in range(pieces):
            scatter.middle(way, b, j)
            if way == 1 and forward:
                gather.step(*forward.pop(0))
    while forward:
        gather.step(*forward.pop(0))
    for j in range(pieces):
        rows = pl.ds(j * sub, sub)
        scatter.last(j, total)
        live = live_mask(length, c * tok + j * sub, sub)
        middle = x_ref[rows].astype(f32) + live * (total[...] + outb_ref[...])
        mid_ref[rows] = middle
        normed, _ = normalize(middle)
        h2_ref[rows] = (normed * gain_ref[...] + shift_ref[...]).astype(bf16)
    for j in range(pieces):
        gather.drain(j)
        for b in range(n):
            scatter.drain(b, j)
    keep.wait()


def attention_forward(
    n, h_all, proj, qb, vb, slopes, length, out_w, x, out_b, gain_two, shift_two, cot
):
    tok, width = x.shape
    slab = proj.shape[2]
    rows = n * tok
    pieces = pieces_of(tok)
    shape = jax.ShapeDtypeStruct
    return pl.pallas_call(
        functools.partial(attention_kernel, n, pieces),
        out_shape=(
            shape((rows, slab), bf16),
            shape((rows, slab), bf16),
            shape((rows, slab), bf16),
            shape((rows, slab), bf16),
            shape((rows, 128), f32),
            shape((tok, width), f32),
            shape((tok, width), bf16),
            shape((rows, width), bf16),
        ),
        in_specs=[VM, VM, VM, VM, SM, SM, VM, VM, VM, VM, VM, VM],
        out_specs=(VM, VM, VM, VM, VM, VM, VM, HB),
        scratch_shapes=[
            pltpu.VMEM((tok, width), bf16),
            pltpu.VMEM((rows, width), bf16),
            pltpu.VMEM((2, rows, width), bf16),
            pltpu.VMEM((tok // pieces, width), f32),
            pltpu.SemaphoreType.DMA((2, n - 1, pieces)),
            pltpu.SemaphoreType.DMA((2, n - 1, pieces)),
            pltpu.SemaphoreType.DMA((2, n, pieces)),
            pltpu.SemaphoreType.DMA((2, n, pieces)),
            pltpu.SemaphoreType.DMA,
        ],
        compiler_params=pltpu.CompilerParams(
            collective_id=2, has_side_effects=True, vmem_limit_bytes=58 * 2**20
        ),
        cost_estimate=pl.CostEstimate(
            flops=2 * rows * width * slab * 4 + 4 * rows * rows * slab,
            bytes_accessed=200 * 2**20,
            transcendentals=rows * rows * slab // 64,
        ),
        name="attention_forward",
    )(h_all, proj, qb, vb, slopes, length, out_w, x, out_b, gain_two, shift_two, cot)


def attention_back_block(
    tok, b, q_ref, k_ref, v_ref, att_ref, lse_ref, ga_ref, dq_ref, dk_acc, dv_acc, slopes_ref, length
):
    pairs = q_ref.shape[1] // 128
    extent = (b + 1) * tok
    rows = pl.ds(b * tok, tok)
    lane = lax.broadcasted_iota(jnp.int32, (tok, 128), 1)

    def pair(p, _):
        lanes = pl.ds(pl.multiple_of(p * 128, 128), 128)
        query = q_ref[rows, lanes]
        grads = ga_ref[rows, lanes]
        keys = k_ref[pl.ds(0, extent), lanes]
        values = v_ref[pl.ds(0, extent), lanes]
        product = grads.astype(f32) * att_ref[rows, lanes].astype(f32)
        lse_all = lse_ref[rows, :]
        dq = []
        dk = None
        dv = None
        for u in (0, 1):
            mine = (lane < 64) if u == 0 else (lane >= 64)
            zero = jnp.zeros_like(query)
            own_query = jnp.where(mine, query, zero)
            own_grads = jnp.where(mine, grads, zero)
            bias = key_bias(slopes_ref[0, 2 * p + u], length, extent)
            scores = masked_scores(own_query, keys, bias, tok, b * tok)
            total = jnp.sum(jnp.where(lane == 2 * p + u, lse_all, 0.0), axis=1, keepdims=True)
            inner = jnp.sum(jnp.where(mine, product, 0.0), axis=1, keepdims=True)
            weights = jnp.exp2(scores - total)
            grad_scores = (weights * (nt(own_grads, values) - inner)).astype(bf16)
            dq.append(nn(grad_scores, keys))
            add_dv = tn(weights.astype(bf16), own_grads)
            add_dk = tn(grad_scores, own_query)
            dv = add_dv if dv is None else dv + add_dv
            dk = add_dk if dk is None else dk + add_dk
        dq_ref[rows, lanes] = (jnp.where(lane < 64, dq[0], dq[1]) * 0.125).astype(bf16)
        past = pl.ds(0, extent)
        dk_acc[past, lanes] += dk
        dv_acc[past, lanes] += dv
        return 0

    lax.fori_loop(0, pairs, pair, 0)


def attention_back_kernel(
    n,
    q_ref,
    k_ref,
    v_ref,
    att_ref,
    lse_ref,
    ga_ref,
    slopes_ref,
    length_ref,
    dq_ref,
    dk_ref,
    dv_ref,
    dk_acc,
    dv_acc,
):
    tok = q_ref.shape[0] // n
    length = length_ref[0]
    dk_acc[...] = jnp.zeros_like(dk_acc)
    dv_acc[...] = jnp.zeros_like(dv_acc)
    for b in reversed(range(n)):
        attention_back_block(
            tok, b, q_ref, k_ref, v_ref, att_ref, lse_ref, ga_ref, dq_ref, dk_acc, dv_acc,
            slopes_ref, length,
        )
        rows = pl.ds(b * tok, tok)
        dk_ref[rows] = dk_acc[rows].astype(bf16)
        dv_ref[rows] = dv_acc[rows].astype(bf16)


def attention_backward(n, q, k, v, att, lse, grad_att, slopes, length):
    rows, slab = q.shape
    shape = jax.ShapeDtypeStruct((rows, slab), bf16)
    return pl.pallas_call(
        functools.partial(attention_back_kernel, n),
        out_shape=(shape, shape, shape),
        in_specs=[VM, VM, VM, VM, VM, VM, SM, SM],
        out_specs=(VM, VM, VM),
        scratch_shapes=[pltpu.VMEM((rows, slab), f32), pltpu.VMEM((rows, slab), f32)],
        compiler_params=pltpu.CompilerParams(vmem_limit_bytes=48 * 2**20),
        cost_estimate=pl.CostEstimate(
            flops=10 * rows * rows * slab, bytes_accessed=100 * 2**20,
            transcendentals=rows * rows * slab // 64,
        ),
        name="attention_backward",
    )(q, k, v, att, lse, grad_att, slopes, length)


def gelu_slope(before):
    cumulative = 0.5 * (1.0 + lax.erf(before * (1.0 / math.sqrt(2.0))))
    density = jnp.exp(-0.5 * before * before) * (1.0 / math.sqrt(2.0 * math.pi))
    return cumulative + before * density


def scatter_rows(partial):
    return lax.psum_scatter(partial, "cols", scatter_dimension=0, tiled=True).astype(f32)


def per_device(
    inputs,
    lengths,
    gain_one,
    shift_one,
    projection,
    query_bias,
    value_bias,
    out_weight,
    out_bias,
    gain_two,
    shift_two,
    up_weight,
    up_bias,
    down_weight,
    down_bias,
    cotangent,
):
    n = lax.axis_size("cols")
    c = lax.axis_index("cols")
    tok, width = inputs.shape
    slab = projection.shape[2]
    heads_here = slab // HEAD_DIM
    head_ids = c * heads_here + jnp.arange(heads_here)
    slopes = jnp.exp2(-8.0 * (head_ids + 1).astype(f32) / HEADS).reshape(1, heads_here)
    live = ((c * tok + jnp.arange(tok)) < lengths[0]).astype(f32)[:, None]

    proj = lax.all_gather(jnp.transpose(projection, (1, 0, 2)), "rows", axis=1, tiled=True)
    out_w = lax.all_gather(out_weight, "rows", axis=1, tiled=True)
    up_w = lax.all_gather(up_weight, "rows", axis=0, tiled=True)
    down_w = lax.all_gather(down_weight, "rows", axis=1, tiled=True)

    h_all = gather_normed(n, inputs, gain_one.reshape(1, -1), shift_one.reshape(1, -1))
    q, k, v, att, lse, middle, h_two, dense = attention_forward(
        n,
        h_all,
        proj,
        query_bias.reshape(1, -1),
        value_bias.reshape(1, -1),
        slopes,
        lengths,
        out_w,
        inputs,
        out_bias.reshape(1, -1),
        gain_two.reshape(1, -1),
        shift_two.reshape(1, -1),
        cotangent,
    )
    h2_all = lax.all_gather(h_two, "cols", axis=0, tiled=True)
    before = nn(h2_all, up_w) + up_bias
    active = jax.nn.gelu(before, approximate=False).astype(bf16)
    dense_out = scatter_rows(nn(active, down_w).astype(bf16)) + down_bias
    output = (middle + live * dense_out).astype(bf16)

    grad_active = nt(dense, down_w)
    grad_before = (grad_active * gelu_slope(before)).astype(bf16)
    down_grad = tn(active, dense)
    up_grad = tn(h2_all, grad_before)
    grad_two = scatter_rows(nt(grad_before, up_w).astype(bf16))
    grad_out = cotangent.astype(f32)
    normed_two, inverse_two = normalize(middle)
    gain_two_part = jnp.sum(grad_two * normed_two, axis=0)
    shift_two_part = jnp.sum(grad_two, axis=0)
    grad_middle = grad_out + norm_back(grad_two, normed_two, inverse_two, gain_two)
    grad_branch = (live * grad_middle).astype(bf16)
    branch_all = lax.all_gather(grad_branch, "cols", axis=0, tiled=True)
    out_grad = tn(att, branch_all)
    grad_att = nt(branch_all, out_w).astype(bf16)
    dq, dk, dv = attention_backward(n, q, k, v, att, lse, grad_att, slopes, lengths)
    proj_grad = jnp.stack([tn(h_all, dq), tn(h_all, dk), tn(h_all, dv)], axis=0)
    grad_one = scatter_rows((nt(dq, proj[0]) + nt(dk, proj[1]) + nt(dv, proj[2])).astype(bf16))
    normed_one, inverse_one = normalize(inputs.astype(f32))
    gain_one_part = jnp.sum(grad_one * normed_one, axis=0)
    shift_one_part = jnp.sum(grad_one, axis=0)
    inputs_grad = grad_middle + norm_back(grad_one, normed_one, inverse_one, gain_one)

    def reduced(grad, dim):
        return lax.psum_scatter(grad.astype(bf16), "rows", scatter_dimension=dim, tiled=True).astype(
            f32
        )

    proj_part = jnp.transpose(reduced(proj_grad, 1), (1, 0, 2))
    up_part = reduced(up_grad, 0)
    out_part = reduced(out_grad, 1)
    down_part = reduced(down_grad, 1)

    query_total, value_total, up_bias_total = lax.psum(
        (
            jnp.sum(dq, axis=0, dtype=f32),
            jnp.sum(dv, axis=0, dtype=f32),
            jnp.sum(grad_before, axis=0, dtype=f32),
        ),
        "rows",
    )
    totals = lax.psum(
        (
            gain_one_part,
            shift_one_part,
            gain_two_part,
            shift_two_part,
            jnp.sum(grad_branch, axis=0, dtype=f32),
            jnp.sum(live * grad_out, axis=0, dtype=f32),
        ),
        ("rows", "cols"),
    )
    gain_one_total, shift_one_total, gain_two_total, shift_two_total, out_b_total, down_b_total = (
        totals
    )
    return (
        output,
        inputs_grad,
        gain_one_total,
        shift_one_total,
        proj_part,
        query_total,
        value_total,
        out_part,
        out_b_total,
        gain_two_total,
        shift_two_total,
        up_part,
        up_bias_total,
        down_part,
        down_b_total,
    )


def solution(mesh):
    rows_cols = P(("rows", "cols"), None)
    return jax.shard_map(
        per_device,
        mesh=mesh,
        in_specs=(
            rows_cols,
            P("rows"),
            P(),
            P(),
            P("rows", None, "cols"),
            P("cols"),
            P("cols"),
            P("cols", "rows"),
            P(),
            P(),
            P(),
            P("rows", "cols"),
            P("cols"),
            P("cols", "rows"),
            P(),
            rows_cols,
        ),
        out_specs=(
            rows_cols,
            rows_cols,
            P(),
            P(),
            P("rows", None, "cols"),
            P("cols"),
            P("cols"),
            P("cols", "rows"),
            P(),
            P(),
            P(),
            P("rows", "cols"),
            P("cols"),
            P("cols", "rows"),
            P(),
        ),
        check_vma=False,
    )
```
